32 devices in a mesh: group: 1, mode: 32 (over z, y, x, core).
Axes of the slice: x: 2, y: 2, z: 4, core: 2. Of those that a mesh axis runs over, the one named last changes fastest.
Arguments:
- source_field: float32 [128, 32, 256], P(('group', 'mode')), may hold values from -650 to 650
- coeff_fields: float32 [11, 32, 256], P('group'), may hold values from 0.5 to 2
- targets: int32 [128, 16], replicated, may hold values from 0 to 31, all different within a row; in each aligned block of 4 rows (0 to 3, 4 to 7, ...) at most 2 rows name the same one
- dest_slot: int32 [128, 16], replicated, may hold values from 0 to 3
- coef_mode: int32 [128, 16], replicated, may hold values from 0 to 10
- coupling: float32 [128, 16], replicated, may hold values from -1 to 1
Outputs:
- first_image: float32 [128, 32, 256], P(('group', 'mode'))
- second_image: float32 [128, 32, 256], P(('group', 'mode'))
The draws below stay inside these ranges and needn't reach their ends.
Inputs may be any that keep to these rules, and one draw needn't show every extreme that they name: `targets`: each row names 16 different owners; the rows j held by one device along `mode` (aligned blocks of 4 rows) name no owner more than 2 times, a bound that some block reaches.
All inputs are finite; a program needn't handle non-finite values.
Results may differ from the reference program's by a relative error of at most 0.000096.
Values sent between devices are 32-bit elements; how exact they have to be, the bound alone decides.
A program may use at most 64 MiB of HBM per device.

```python
import math
import jax
import jax.numpy as jnp
import numpy as np
from jax import lax

MODE_DEV = 4
TOP = 16
NCOEF = 11
GR = 32
GC = 256
MODES = 128
CAP = 2
N_MODE = 32


def draw_source_field(key, part):
    key = jax.random.fold_in(key, 11)
    noise_key, row_key = jax.random.split(key, 2)
    field_shape = (MODES, GR, GC)
    level = jnp.arange(MODES, dtype=jnp.float32) / (MODES - 1)
    row_level = jax.random.uniform(row_key, (1, GR, 1), jnp.float32)
    spread_level = level
    noise = jax.random.truncated_normal(noise_key, -6.0, 6.0, field_shape, jnp.float32)
    return noise * (10.0 ** spread_level)[:, None, None] * 10.0 ** row_level / 3.0


def with_ends(values, own_key, low, top_value):
    extent = values.shape
    index_at = [jax.random.randint(jax.random.fold_in(own_key, axis), (), 0, extent[axis]) for axis in range(len(extent))]
    values = values.at[tuple(index_at)].set(low)
    longest = extent.index(max(extent))
    index_at[longest] = (index_at[longest] + 1) % extent[longest]
    return values.at[tuple(index_at)].set(top_value)


def deal_out(key, own, number, rows, count, top, most, skew):
    sequence = jax.random.permutation(key, count)
    packed, ordinary = load_shares(count, rows * top, most, skew, True), load_shares(count, rows * top, most, skew, False)
    places = jnp.arange(count)

    def named(lengths, offset_by):
        used = int((lengths > 0).sum())
        fixed = max(1, used // 4)
        moved = fixed + (places - fixed + offset_by * (used - fixed)) % max(1, count - fixed)
        return jnp.zeros((count,), jnp.int32).at[sequence[jnp.where(places < fixed, places, moved)]].set(jnp.asarray(lengths, jnp.int32))

    lengths = jnp.where(number % 4 == 0, named(packed, number // 4), named(ordinary, number - number // 4 - 1))
    mixed = jax.random.permutation(jax.random.fold_in(own, 3), count)
    giver, taker = mixed[0:count // 2 * 2:2], mixed[1:count // 2 * 2:2]
    slack = jnp.minimum(lengths[giver] - 1, most - lengths[taker]) // 2
    slack = jnp.where((giver == sequence[0]) | (taker == sequence[0]) | (lengths[taker] == 0), 0, jnp.maximum(slack, 0))
    moved = jax.random.randint(jax.random.fold_in(own, 4), (count // 2,), 0, 1 << 20) % (slack + 1)
    lengths = lengths.at[giver].add(-moved).at[taker].add(moved)
    members = jnp.searchsorted(jnp.cumsum(lengths), jnp.arange(rows * top), side="right").astype(jnp.int32)
    table = members.reshape(top, rows).T
    table = table[jax.random.permutation(jax.random.fold_in(own, 1), rows)]
    offset_by = jax.random.randint(jax.random.fold_in(own, 2), (rows, 1), 0, top)
    return jnp.take_along_axis(table, (jnp.arange(top)[None, :] + offset_by) % top, axis=1)


def load_shares(amount, total, bound, skew, full):
    portions = [(1 << 20) // math.isqrt(rank ** skew) + 1 for rank in range(1, amount + 1)]
    largest = bound if full else min(bound, max(-(-total // amount), total * portions[0] // sum(portions)))
    least = 1 if total - largest >= amount - 1 else 0
    counts, spare = [largest] + [least] * (amount - 1), total - largest - least * (amount - 1)
    while spare > 0:
        candidates = [i for i in range(1, amount) if counts[i] < largest] or [i for i in range(1, amount) if counts[i] < bound]
        whole, left = sum([portions[i] for i in candidates]), spare
        for i in candidates:
            more = min(bound - counts[i], max(1, left * portions[i] // whole), spare)
            counts[i] = counts[i] + more
            spare = spare - more
    return np.array(counts)


def normal_values(stream_key, extent, spread, bound, kind=jnp.bfloat16):
    return jnp.clip(spread * jax.random.normal(stream_key, extent, jnp.float32), -bound, bound).astype(kind)


def setup_inputs(seed: int = 0, part: int = 0) -> dict:
    arg_keys = jax.random.split(jax.random.key(seed), 7)
    part_splits = jax.random.split(jax.random.fold_in(arg_keys[6], part), 7)
    source_field = draw_source_field(jax.random.fold_in(jax.random.fold_in(arg_keys[6], part), 71), part)
    coeff_fields = jnp.clip(jax.random.uniform(part_splits[1], (NCOEF, GR, GC), jnp.float32, 0.5, 2.0), 0.5, 2.0)
    targets_keys = jax.random.split(jax.random.fold_in(arg_keys[2], 1), MODES // MODE_DEV)
    targets_turns = jax.random.permutation(jax.random.fold_in(arg_keys[2], 3), MODES // MODE_DEV)
    targets = jax.vmap(lambda own, number: deal_out(jax.random.fold_in(arg_keys[2], 2), own, number, MODE_DEV, N_MODE, TOP, CAP, 2))(targets_keys, targets_turns).reshape((MODES, TOP))
    dest_slot = with_ends(jax.random.randint(arg_keys[3], (MODES, TOP), 0, MODE_DEV), jax.random.fold_in(arg_keys[3], 1), 0, MODE_DEV - 1).astype(jnp.int32)
    coef_mode = with_ends(jax.random.randint(arg_keys[4], (MODES, TOP), 0, NCOEF), jax.random.fold_in(arg_keys[4], 1), 0, NCOEF - 1).astype(jnp.int32)
    coupling = normal_values(arg_keys[5], (MODES, TOP), (0.25 * TOP ** -0.5), 1.0, jnp.float32)
    return dict(source_field=source_field, coeff_fields=coeff_fields, targets=targets, dest_slot=dest_slot, coef_mode=coef_mode, coupling=coupling)


def laplace(fields):
    padded = jnp.pad(fields, ((0, 0), (1, 1), (1, 1)))
    return 4.0 * fields - padded[:, 2:, 1:-1] - padded[:, :-2, 1:-1] - padded[:, 1:-1, 2:] - padded[:, 1:-1, :-2]

def galerkin(fields, coeff_fields, couplings):
    stencil = laplace(fields).reshape(MODES, GR * GC)
    mixture = jnp.einsum('kji,jc->kic', couplings, stencil, precision=lax.Precision.HIGHEST)
    flat_coeff = coeff_fields.reshape(NCOEF, GR * GC)
    result = lax.optimization_barrier(jnp.sum(mixture * flat_coeff[None], axis=1))
    return result.reshape(MODES, GR, GC)

def reference(source_field, coeff_fields, targets, dest_slot, coef_mode, coupling):
    out_mode = (targets * MODE_DEV + dest_slot).astype(jnp.int32)
    source_rows = jnp.broadcast_to(jnp.arange(MODES, dtype=jnp.int32)[:, None], (MODES, TOP))
    couplings = jnp.zeros((MODES, MODES, NCOEF), jnp.float32)
    couplings = couplings.at[out_mode, source_rows, coef_mode.astype(jnp.int32)].add(coupling)
    energy = jnp.sum(source_field * source_field)
    field_scale = jnp.sqrt(energy / (MODES * GR * GC) + 1e-06)
    start_field = source_field / field_scale
    first_image = galerkin(start_field, coeff_fields, couplings)
    second_image = galerkin(first_image, coeff_fields, couplings)
    return (first_image, second_image)
```

```python
import functools

import jax
import jax.numpy as jnp
from jax import lax
from jax.experimental import pallas as pl
from jax.experimental.pallas import tpu as pltpu
from jax.sharding import PartitionSpec as P

LANES = 128
SUB = 8
MESH = pl.DeviceIdType.MESH


def laplace(fields):
    padded = jnp.pad(fields, ((0, 0), (1, 1), (1, 1)))
    return (
        4.0 * fields
        - padded[:, 2:, 1:-1]
        - padded[:, :-2, 1:-1]
        - padded[:, 1:-1, 2:]
        - padded[:, 1:-1, :-2]
    )


def local_general(source_field, coeff_fields, targets, dest_slot, coef_mode, coupling):
    local_modes, grid_rows, grid_cols = source_field.shape
    cell_count = grid_rows * grid_cols
    devices = lax.axis_size("mode")
    own_index = lax.axis_index("mode")
    coef_count = coeff_fields.shape[0]
    fan_out = targets.shape[1]
    entries = local_modes * fan_out
    slot_count = max(2, -(-entries // devices))
    highest = lax.Precision.HIGHEST
    flat_coeff = coeff_fields.reshape(coef_count, cell_count)
    mode_iota = jnp.arange(local_modes, dtype=jnp.int32)
    coef_iota = jnp.arange(coef_count, dtype=jnp.int32)
    owner_iota = jnp.arange(devices, dtype=jnp.int32)
    first_row = own_index * local_modes
    own_targets = lax.dynamic_slice_in_dim(targets, first_row, local_modes, 0).reshape(entries)
    own_coef = lax.dynamic_slice_in_dim(coef_mode, first_row, local_modes, 0).reshape(entries)
    own_value = lax.dynamic_slice_in_dim(coupling, first_row, local_modes, 0).reshape(entries)

    def local_products(fields):
        stencil = laplace(fields).reshape(local_modes, cell_count)
        coef_hot = (own_coef[:, None] == coef_iota[None, :]).astype(jnp.float32)
        picked = jnp.dot(coef_hot, flat_coeff, precision=highest)
        stencil_rows = jnp.repeat(stencil, fan_out, axis=0)
        return own_value[:, None] * stencil_rows * picked

    def apply_galerkin(fields):
        products = local_products(fields)
        owner_hot = (own_targets[:, None] == owner_iota[None, :]).astype(jnp.int32)
        slot_rank = jnp.sum((jnp.cumsum(owner_hot, axis=0) - owner_hot) * owner_hot, axis=1)
        slot_place = own_targets * slot_count + slot_rank
        packing = (
            jnp.arange(devices * slot_count, dtype=jnp.int32)[:, None] == slot_place[None, :]
        ).astype(jnp.float32)
        outgoing = jnp.dot(packing, products, precision=highest).reshape(
            devices, slot_count, cell_count
        )
        incoming = lax.all_to_all(outgoing, "mode", split_axis=0, concat_axis=0, tiled=True)
        all_targets = targets.reshape(devices, entries)
        all_dest = dest_slot.reshape(devices, entries)
        all_hot = (all_targets[..., None] == owner_iota).astype(jnp.int32)
        all_rank = jnp.sum((jnp.cumsum(all_hot, axis=1) - all_hot) * all_hot, axis=2)
        owned_here = (all_targets == own_index).astype(jnp.float32)
        dest_hot = (all_dest[..., None] == mode_iota).astype(jnp.float32) * owned_here[..., None]
        rank_hot = (all_rank[..., None] == jnp.arange(slot_count, dtype=jnp.int32)).astype(
            jnp.float32
        )
        collect = jnp.einsum("sem,sec->msc", dest_hot, rank_hot, precision=highest)
        collect = collect.reshape(local_modes, devices * slot_count)
        result = jnp.dot(
            collect, incoming.reshape(devices * slot_count, cell_count), precision=highest
        )
        return result.reshape(local_modes, grid_rows, grid_cols)

    energy = lax.psum(jnp.sum(source_field * source_field), "mode")
    field_scale = jnp.sqrt(energy / (targets.shape[0] * cell_count) + 1e-06)
    start_field = source_field / field_scale
    first_image = apply_galerkin(start_field)
    second_image = apply_galerkin(first_image)
    return (first_image, second_image)


def row_of(device):
    core = device % 2
    chip = device // 2
    x = chip % 2
    y = (chip // 2) % 2
    z = chip // 4
    place = y * 2 + (x + y) % 2
    odd = z % 2
    place = place + odd * (3 - 2 * place)
    return (z * 4 + place) * 2 + core


def device_of(row):
    core = row % 2
    step = row // 2
    z = step // 4
    place = step % 4
    odd = z % 2
    place = place + odd * (3 - 2 * place)
    y = place // 2
    x = (place + y) % 2
    return ((z * 2 + y) * 2 + x) * 2 + core


def split(values):
    high = values.astype(jnp.bfloat16)
    return high, (values - high.astype(jnp.float32)).astype(jnp.bfloat16)


def side_sum(field):
    cols = field.shape[1]
    place = lax.broadcasted_iota(jnp.int32, field.shape, 1)
    left = jnp.where(place == 0, 0.0, pltpu.roll(field, 1, 1))
    right = jnp.where(place == cols - 1, 0.0, pltpu.roll(field, cols - 1, 1))
    return left + right


def end_sum(field):
    rows = field.shape[0]
    place = lax.broadcasted_iota(jnp.int32, field.shape, 0)
    upper = jnp.where(place == 0, 0.0, pltpu.roll(field, 1, 0))
    lower = jnp.where(place == rows - 1, 0.0, pltpu.roll(field, rows - 1, 0))
    return upper + lower


def kernel(
    n, cell_total,
    source, coeff, targets, dest, coef_mode, coupling,
    first, second,
    out_a, in_a, out_b, in_b, out_c, in_c, e_out, e_in, mine, above, below, a_high, a_low,
    send_a, recv_a, send_b, recv_b, send_c, recv_c, send_e, recv_e, send_h, recv_h,
):
    modes_dev, rows, cols = source.shape
    terms = coeff.shape[0]
    modes, top = targets.shape
    halves = cols // LANES
    me = lax.axis_index("mode")
    row = row_of(me)

    barrier = pltpu.get_barrier_semaphore()

    def greet(step, _):
        pl.semaphore_signal(
            barrier, inc=1, device_id={"mode": lax.rem(me + step, n)}, device_id_type=MESH
        )
        return 0

    lax.fori_loop(1, n, greet, 0)

    def tile(buf, index):
        return buf.at[pl.ds(pl.multiple_of(index * SUB, SUB), SUB), :]

    energy = jnp.zeros((1, LANES), jnp.float32)
    for m in range(modes_dev):
        field = source[m]
        stencil = 4.0 * field - end_sum(field) - side_sum(field)
        squares = jnp.sum(field * field, axis=0, keepdims=True)
        for h in range(halves):
            out_a[pl.ds(h * modes_dev + m, rows, stride=SUB), :] = stencil[:, h * LANES:(h + 1) * LANES]
            energy = energy + squares[:, h * LANES:(h + 1) * LANES]
    e_out[...] = energy

    pl.semaphore_wait(barrier, n - 1)

    def send_rows(step, _):
        other = lax.rem(me + step, n)
        pltpu.make_async_remote_copy(
            src_ref=tile(out_a, row_of(other)), dst_ref=tile(in_a, me),
            send_sem=send_a, recv_sem=recv_a,
            device_id={"mode": other}, device_id_type=MESH,
        ).start()
        return 0

    def send_energy(step, _):
        other = lax.rem(me + step, n)
        pltpu.make_async_remote_copy(
            src_ref=e_out, dst_ref=e_in.at[me],
            send_sem=send_e, recv_sem=recv_e,
            device_id={"mode": other}, device_id_type=MESH,
        ).start()
        return 0

    lax.fori_loop(1, n, send_rows, 0)
    lax.fori_loop(1, n, send_energy, 0)
    in_a[pl.ds(pl.multiple_of(me * SUB, SUB), SUB), :] = out_a[pl.ds(pl.multiple_of(row * SUB, SUB), SUB), :]
    e_in[me] = energy

    j_iota = lax.broadcasted_iota(jnp.int32, (modes, modes), 0)
    p_iota = lax.broadcasted_iota(jnp.int32, (modes, modes), 1)
    order = jnp.where((j_iota % modes_dev) * n + j_iota // modes_dev == p_iota, 1.0, 0.0)

    def reordered(values):
        return lax.dot_general(
            values, order, (((0,), (0,)), ((), ())),
            precision=lax.Precision.HIGHEST, preferred_element_type=jnp.float32,
        )

    place_t = reordered((dest[...] * n + targets[...]).astype(jnp.float32))
    coef_t = reordered(coef_mode[...].astype(jnp.float32))
    value_t = reordered(coupling[...])
    k_iota = j_iota.astype(jnp.float32)
    value = jnp.zeros((modes, modes), jnp.float32)
    index = jnp.zeros((modes, modes), jnp.float32)
    for t in range(top):
        hit = place_t[t:t + 1, :] == k_iota
        value = jnp.where(hit, value_t[t:t + 1, :], value)
        index = jnp.where(hit, coef_t[t:t + 1, :], index)
    for i in range(terms):
        high, low = split(jnp.where(index == float(i), value, 0.0))
        rows_i = pl.ds(i * modes, modes)
        a_high[rows_i, :modes] = high
        a_high[rows_i, modes:] = high
        a_low[rows_i, :] = low

    def galerkin(stencil):
        high, low = split(stencil)
        both = jnp.concatenate([high, low], axis=0)
        total = jnp.zeros((modes, cols), jnp.float32)
        for i in range(terms):
            rows_i = pl.ds(i * modes, modes)
            mixture = jnp.dot(a_high[rows_i, :], both, preferred_element_type=jnp.float32)
            mixture = mixture + jnp.dot(a_low[rows_i, :], high, preferred_element_type=jnp.float32)
            total = total + coeff[i, pl.ds(row, 1), :] * mixture
        return total

    def wait_all(out_buf, in_buf, send, recv):
        count = pl.ds(0, (n - 1) * SUB)
        pltpu.make_async_copy(out_buf.at[count, :], out_buf.at[count, :], send).wait()
        pltpu.make_async_copy(in_buf.at[count, :], in_buf.at[count, :], recv).wait()

    wait_all(out_a, in_a, send_a, recv_a)
    stencil = jnp.concatenate(
        [
            jnp.concatenate(
                [in_a[pl.ds(h * modes_dev + m, n, stride=SUB), :] for h in range(halves)], axis=1
            )
            for m in range(modes_dev)
        ],
        axis=0,
    )
    image = galerkin(stencil)
    others = pl.ds(0, n - 1)
    pltpu.make_async_copy(e_in.at[others], e_in.at[others], recv_e).wait()
    pltpu.make_async_copy(e_in.at[others], e_in.at[others], send_e).wait()
    whole = jnp.sum(jnp.sum(e_in[...], axis=0), axis=1, keepdims=True)
    image = image / jnp.sqrt(whole / cell_total + 1e-06)
    mine[...] = image

    def halo(there, slot, sem):
        return pltpu.make_async_remote_copy(
            src_ref=mine, dst_ref=slot, send_sem=send_h.at[sem], recv_sem=recv_h.at[sem],
            device_id={"mode": device_of(there)}, device_id_type=MESH,
        )

    @pl.when(row < rows - 1)
    def _():
        halo(row + 1, above, 0).start()

    @pl.when(row > 0)
    def _():
        halo(row - 1, below, 1).start()

    def place_tiles(buf, values):
        for m in range(modes_dev):
            for h in range(halves):
                buf[pl.ds(h * modes_dev + m, n, stride=SUB), :] = values[
                    m * n:(m + 1) * n, h * LANES:(h + 1) * LANES
                ]

    def send_back(out_buf, in_buf, send, recv):
        def body(step, _):
            other = lax.rem(me + step, n)
            pltpu.make_async_remote_copy(
                src_ref=tile(out_buf, other), dst_ref=tile(in_buf, row),
                send_sem=send, recv_sem=recv,
                device_id={"mode": other}, device_id_type=MESH,
            ).start()
            return 0

        lax.fori_loop(1, n, body, 0)
        in_buf[pl.ds(pl.multiple_of(row * SUB, SUB), SUB), :] = out_buf[
            pl.ds(pl.multiple_of(me * SUB, SUB), SUB), :
        ]

    def take_tiles(buf, result):
        for m in range(modes_dev):
            for h in range(halves):
                result[m, :, h * LANES:(h + 1) * LANES] = buf[pl.ds(h * modes_dev + m, rows, stride=SUB), :]

    place_tiles(out_b, image)
    send_back(out_b, in_b, send_b, recv_b)

    inner = 4.0 * image - side_sum(image)

    @pl.when(row == 0)
    def _():
        above[...] = jnp.zeros_like(above)

    @pl.when(row == rows - 1)
    def _():
        below[...] = jnp.zeros_like(below)

    @pl.when(row > 0)
    def _():
        halo(row - 1, above, 0).wait_recv()

    @pl.when(row < rows - 1)
    def _():
        halo(row + 1, below, 1).wait_recv()

    image = galerkin(inner - above[...] - below[...])
    place_tiles(out_c, image)
    send_back(out_c, in_c, send_c, recv_c)

    wait_all(out_b, in_b, send_b, recv_b)
    take_tiles(in_b, first)

    @pl.when(row < rows - 1)
    def _():
        halo(row + 1, above, 0).wait_send()

    @pl.when(row > 0)
    def _():
        halo(row - 1, below, 1).wait_send()

    wait_all(out_c, in_c, send_c, recv_c)
    take_tiles(in_c, second)


def local_rows(source_field, coeff_fields, targets, dest_slot, coef_mode, coupling):
    modes_dev, rows, cols = source_field.shape
    n = lax.axis_size("mode")
    modes = targets.shape[0]
    terms = coeff_fields.shape[0]
    tiles = pltpu.VMEM((n * SUB, LANES), jnp.float32)
    grid_row = pltpu.VMEM((modes, cols), jnp.float32)
    image = jax.ShapeDtypeStruct(source_field.shape, jnp.float32)
    in_vmem = pl.BlockSpec(memory_space=pltpu.VMEM)
    dma = pltpu.SemaphoreType.DMA
    return pl.pallas_call(
        functools.partial(kernel, n, float(modes * rows * cols)),
        out_shape=(image, image),
        in_specs=[in_vmem] * 6,
        out_specs=(in_vmem, in_vmem),
        scratch_shapes=[tiles] * 6
        + [
            pltpu.VMEM((1, LANES), jnp.float32),
            pltpu.VMEM((n, 1, LANES), jnp.float32),
            grid_row, grid_row, grid_row,
            pltpu.VMEM((terms * modes, 2 * modes), jnp.bfloat16),
            pltpu.VMEM((terms * modes, modes), jnp.bfloat16),
        ]
        + [dma] * 8 + [dma((2,)), dma((2,))],
        compiler_params=pltpu.CompilerParams(
            collective_id=0, has_side_effects=True, vmem_limit_bytes=32 * 1024 * 1024
        ),
    )(source_field, coeff_fields, targets, dest_slot, coef_mode, coupling)


def local(source_field, *rest):
    modes_dev, rows, cols = source_field.shape
    n = lax.axis_size("mode")
    if n == rows and n % SUB == 0 and cols % LANES == 0 and modes_dev * (cols // LANES) == SUB:
        return local_rows(source_field, *rest)
    return local_general(source_field, *rest)


def solution(mesh):
    in_specs = (P(("group", "mode"), None, None), P("group", None, None), P(), P(), P(), P())
    out_specs = (P(("group", "mode"), None, None), P(("group", "mode"), None, None))
    return jax.shard_map(local, mesh=mesh, in_specs=in_specs, out_specs=out_specs, check_vma=False)
```

```python
import functools

import jax
import jax.numpy as jnp
from jax import lax
from jax.experimental import pallas as pl
from jax.experimental.pallas import tpu as pltpu
from jax.sharding import PartitionSpec as P

LANES = 128
SUB = 8
MESH = pl.DeviceIdType.MESH


def laplace(fields):
    padded = jnp.pad(fields, ((0, 0), (1, 1), (1, 1)))
    return (
        4.0 * fields
        - padded[:, 2:, 1:-1]
        - padded[:, :-2, 1:-1]
        - padded[:, 1:-1, 2:]
        - padded[:, 1:-1, :-2]
    )


def local_general(source_field, coeff_fields, targets, dest_slot, coef_mode, coupling):
    local_modes, grid_rows, grid_cols = source_field.shape
    cell_count = grid_rows * grid_cols
    devices = lax.axis_size("mode")
    own_index = lax.axis_index("mode")
    coef_count = coeff_fields.shape[0]
    fan_out = targets.shape[1]
    entries = local_modes * fan_out
    slot_count = max(2, -(-entries // devices))
    highest = lax.Precision.HIGHEST
    flat_coeff = coeff_fields.reshape(coef_count, cell_count)
    mode_iota = jnp.arange(local_modes, dtype=jnp.int32)
    coef_iota = jnp.arange(coef_count, dtype=jnp.int32)
    owner_iota = jnp.arange(devices, dtype=jnp.int32)
    first_row = own_index * local_modes
    own_targets = lax.dynamic_slice_in_dim(targets, first_row, local_modes, 0).reshape(entries)
    own_coef = lax.dynamic_slice_in_dim(coef_mode, first_row, local_modes, 0).reshape(entries)
    own_value = lax.dynamic_slice_in_dim(coupling, first_row, local_modes, 0).reshape(entries)

    def local_products(fields):
        stencil = laplace(fields).reshape(local_modes, cell_count)
        coef_hot = (own_coef[:, None] == coef_iota[None, :]).astype(jnp.float32)
        picked = jnp.dot(coef_hot, flat_coeff, precision=highest)
        stencil_rows = jnp.repeat(stencil, fan_out, axis=0)
        return own_value[:, None] * stencil_rows * picked

    def apply_galerkin(fields):
        products = local_products(fields)
        owner_hot = (own_targets[:, None] == owner_iota[None, :]).astype(jnp.int32)
        slot_rank = jnp.sum((jnp.cumsum(owner_hot, axis=0) - owner_hot) * owner_hot, axis=1)
        slot_place = own_targets * slot_count + slot_rank
        packing = (
            jnp.arange(devices * slot_count, dtype=jnp.int32)[:, None] == slot_place[None, :]
        ).astype(jnp.float32)
        outgoing = jnp.dot(packing, products, precision=highest).reshape(
            devices, slot_count, cell_count
        )
        incoming = lax.all_to_all(outgoing, "mode", split_axis=0, concat_axis=0, tiled=True)
        all_targets = targets.reshape(devices, entries)
        all_dest = dest_slot.reshape(devices, entries)
        all_hot = (all_targets[..., None] == owner_iota).astype(jnp.int32)
        all_rank = jnp.sum((jnp.cumsum(all_hot, axis=1) - all_hot) * all_hot, axis=2)
        owned_here = (all_targets == own_index).astype(jnp.float32)
        dest_hot = (all_dest[..., None] == mode_iota).astype(jnp.float32) * owned_here[..., None]
        rank_hot = (all_rank[..., None] == jnp.arange(slot_count, dtype=jnp.int32)).astype(
            jnp.float32
        )
        collect = jnp.einsum("sem,sec->msc", dest_hot, rank_hot, precision=highest)
        collect = collect.reshape(local_modes, devices * slot_count)
        result = jnp.dot(
            collect, incoming.reshape(devices * slot_count, cell_count), precision=highest
        )
        return result.reshape(local_modes, grid_rows, grid_cols)

    energy = lax.psum(jnp.sum(source_field * source_field), "mode")
    field_scale = jnp.sqrt(energy / (targets.shape[0] * cell_count) + 1e-06)
    start_field = source_field / field_scale
    first_image = apply_galerkin(start_field)
    second_image = apply_galerkin(first_image)
    return (first_image, second_image)


def row_of(device):
    core = device % 2
    chip = device // 2
    x = chip % 2
    y = (chip // 2) % 2
    z = chip // 4
    place = y * 2 + (x + y) % 2
    odd = z % 2
    place = place + odd * (3 - 2 * place)
    return (z * 4 + place) * 2 + core


def device_of(row):
    core = row % 2
    step = row // 2
    z = step // 4
    place = step % 4
    odd = z % 2
    place = place + odd * (3 - 2 * place)
    y = place // 2
    x = (place + y) % 2
    return ((z * 2 + y) * 2 + x) * 2 + core


def split(values):
    high = values.astype(jnp.bfloat16)
    return high, (values - high.astype(jnp.float32)).astype(jnp.bfloat16)


def side_sum(field):
    cols = field.shape[1]
    place = lax.broadcasted_iota(jnp.int32, field.shape, 1)
    left = jnp.where(place == 0, 0.0, pltpu.roll(field, 1, 1))
    right = jnp.where(place == cols - 1, 0.0, pltpu.roll(field, cols - 1, 1))
    return left + right


def end_sum(field):
    rows = field.shape[0]
    place = lax.broadcasted_iota(jnp.int32, field.shape, 0)
    upper = jnp.where(place == 0, 0.0, pltpu.roll(field, 1, 0))
    lower = jnp.where(place == rows - 1, 0.0, pltpu.roll(field, rows - 1, 0))
    return upper + lower


def kernel(
    n, cell_total,
    source_hbm, coeff_hbm, targets_hbm, dest_hbm, coef_mode_hbm, coupling_hbm,
    first, second,
    source, coeff, targets, dest, coef_mode, coupling,
    out_a, in_a, out_b, in_b, out_c, in_c, e_out, e_in, mine, above, below, a_high, a_low,
    send_a, recv_a, send_b, recv_b, send_c, recv_c, send_e, recv_e, send_h, recv_h, load_source, load_rest,
):
    modes_dev, rows, cols = source.shape
    terms = coeff.shape[0]
    top, modes = targets.shape
    halves = cols // LANES
    me = lax.axis_index("mode")
    row = row_of(me)
    block = pl.multiple_of(row // SUB * SUB, SUB)

    loads = [pltpu.make_async_copy(source_hbm, source, load_source)]
    pairs = (
        (targets_hbm, targets), (dest_hbm, dest), (coef_mode_hbm, coef_mode), (coupling_hbm, coupling),
        (coeff_hbm.at[:, pl.ds(block, SUB), :], coeff),
    )
    loads += [pltpu.make_async_copy(src, dst, load_rest.at[k]) for k, (src, dst) in enumerate(pairs)]
    for load in loads:
        load.start()

    barrier = pltpu.get_barrier_semaphore()

    def greet(step, _):
        pl.semaphore_signal(
            barrier, inc=1, device_id={"mode": lax.rem(me + step, n)}, device_id_type=MESH
        )
        return 0

    lax.fori_loop(1, n, greet, 0)

    def tile(buf, index):
        return buf.at[pl.ds(pl.multiple_of(index * SUB, SUB), SUB), :]

    loads[0].wait()
    energy = jnp.zeros((1, LANES), jnp.float32)
    for m in range(modes_dev):
        field = source[m]
        stencil = 4.0 * field - end_sum(field) - side_sum(field)
        squares = jnp.sum(field * field, axis=0, keepdims=True)
        for h in range(halves):
            out_a[pl.ds(h * modes_dev + m, rows, stride=SUB), :] = stencil[:, h * LANES:(h + 1) * LANES]
            energy = energy + squares[:, h * LANES:(h + 1) * LANES]
    e_out[...] = energy

    pl.semaphore_wait(barrier, n - 1)

    def send_rows(step, _):
        other = lax.rem(me + step, n)
        pltpu.make_async_remote_copy(
            src_ref=tile(out_a, row_of(other)), dst_ref=tile(in_a, me),
            send_sem=send_a, recv_sem=recv_a,
            device_id={"mode": other}, device_id_type=MESH,
        ).start()
        return 0

    def send_energy(step, _):
        other = lax.rem(me + step, n)
        pltpu.make_async_remote_copy(
            src_ref=e_out, dst_ref=e_in.at[me],
            send_sem=send_e, recv_sem=recv_e,
            device_id={"mode": other}, device_id_type=MESH,
        ).start()
        return 0

    lax.fori_loop(1, n, send_rows, 0)
    e_in[me] = energy
    in_a[pl.ds(pl.multiple_of(me * SUB, SUB), SUB), :] = out_a[pl.ds(pl.multiple_of(row * SUB, SUB), SUB), :]

    for load in loads[1:]:
        load.wait()
    j_iota = lax.broadcasted_iota(jnp.int32, (modes, modes), 0)
    p_iota = lax.broadcasted_iota(jnp.int32, (modes, modes), 1)
    order = jnp.where((j_iota % modes_dev) * n + j_iota // modes_dev == p_iota, 1.0, 0.0)

    def reordered(values):
        return lax.dot_general(
            values, order, (((1,), (0,)), ((), ())),
            precision=lax.Precision.HIGHEST, preferred_element_type=jnp.float32,
        )

    place_t = reordered((dest[...] * n + targets[...]).astype(jnp.float32))
    coef_t = reordered(coef_mode[...].astype(jnp.float32))
    value_t = reordered(coupling[...])
    k_iota = j_iota.astype(jnp.float32)
    value = jnp.zeros((modes, modes), jnp.float32)
    index = jnp.zeros((modes, modes), jnp.float32)
    for t in range(top):
        hit = place_t[t:t + 1, :] == k_iota
        value = jnp.where(hit, value_t[t:t + 1, :], value)
        index = jnp.where(hit, coef_t[t:t + 1, :], index)
    for i in range(terms):
        high, low = split(jnp.where(index == float(i), value, 0.0))
        rows_i = pl.ds(i * modes, modes)
        a_high[rows_i, :modes] = high
        a_high[rows_i, modes:] = high
        a_low[rows_i, :] = low

    def galerkin(stencil):
        high, low = split(stencil)
        both = jnp.concatenate([high, low], axis=0)
        total = jnp.zeros((modes, cols), jnp.float32)
        for i in range(terms):
            rows_i = pl.ds(i * modes, modes)
            mixture = jnp.dot(a_high[rows_i, :], both, preferred_element_type=jnp.float32)
            mixture = mixture + jnp.dot(a_low[rows_i, :], high, preferred_element_type=jnp.float32)
            total = total + coeff[i, pl.ds(row - block, 1), :] * mixture
        return total

    def wait_all(out_buf, in_buf, send, recv):
        count = pl.ds(0, (n - 1) * SUB)
        pltpu.make_async_copy(out_buf.at[count, :], out_buf.at[count, :], send).wait()
        pltpu.make_async_copy(in_buf.at[count, :], in_buf.at[count, :], recv).wait()

    wait_all(out_a, in_a, send_a, recv_a)
    stencil = jnp.concatenate(
        [
            jnp.concatenate(
                [in_a[pl.ds(h * modes_dev + m, n, stride=SUB), :] for h in range(halves)], axis=1
            )
            for m in range(modes_dev)
        ],
        axis=0,
    )
    image = galerkin(stencil)
    mine[...] = image

    def halo(there, slot, sem):
        return pltpu.make_async_remote_copy(
            src_ref=mine, dst_ref=slot, send_sem=send_h.at[sem], recv_sem=recv_h.at[sem],
            device_id={"mode": device_of(there)}, device_id_type=MESH,
        )

    @pl.when(row < rows - 1)
    def _():
        halo(row + 1, above, 0).start()

    @pl.when(row > 0)
    def _():
        halo(row - 1, below, 1).start()

    def place_tiles(buf, values):
        for m in range(modes_dev):
            for h in range(halves):
                buf[pl.ds(h * modes_dev + m, n, stride=SUB), :] = values[
                    m * n:(m + 1) * n, h * LANES:(h + 1) * LANES
                ]

    def send_back(out_buf, in_buf, send, recv):
        def body(step, _):
            other = lax.rem(me + step, n)
            pltpu.make_async_remote_copy(
                src_ref=tile(out_buf, other), dst_ref=tile(in_buf, row),
                send_sem=send, recv_sem=recv,
                device_id={"mode": other}, device_id_type=MESH,
            ).start()
            return 0

        lax.fori_loop(1, n, body, 0)
        in_buf[pl.ds(pl.multiple_of(row * SUB, SUB), SUB), :] = out_buf[
            pl.ds(pl.multiple_of(me * SUB, SUB), SUB), :
        ]

    def take_tiles(buf, result):
        for m in range(modes_dev):
            for h in range(halves):
                result[m, :, h * LANES:(h + 1) * LANES] = buf[
                    pl.ds(h * modes_dev + m, rows, stride=SUB), :
                ] * scale

    place_tiles(out_b, image)
    send_back(out_b, in_b, send_b, recv_b)

    lax.fori_loop(1, n, send_energy, 0)
    inner = 4.0 * image - side_sum(image)

    @pl.when(row == 0)
    def _():
        above[...] = jnp.zeros_like(above)

    @pl.when(row == rows - 1)
    def _():
        below[...] = jnp.zeros_like(below)

    @pl.when(row > 0)
    def _():
        halo(row - 1, above, 0).wait_recv()

    @pl.when(row < rows - 1)
    def _():
        halo(row + 1, below, 1).wait_recv()

    image = galerkin(inner - above[...] - below[...])
    place_tiles(out_c, image)
    send_back(out_c, in_c, send_c, recv_c)

    wait_all(out_b, in_b, send_b, recv_b)
    others = pl.ds(0, n - 1)
    pltpu.make_async_copy(e_in.at[others], e_in.at[others], recv_e).wait()
    pltpu.make_async_copy(e_in.at[others], e_in.at[others], send_e).wait()
    whole = jnp.sum(jnp.sum(e_in[...], axis=0), axis=1, keepdims=True)
    scale = 1.0 / jnp.sqrt(whole / cell_total + 1e-06)
    take_tiles(in_b, first)

    @pl.when(row < rows - 1)
    def _():
        halo(row + 1, above, 0).wait_send()

    @pl.when(row > 0)
    def _():
        halo(row - 1, below, 1).wait_send()

    wait_all(out_c, in_c, send_c, recv_c)
    take_tiles(in_c, second)


def local_rows(source_field, coeff_fields, targets, dest_slot, coef_mode, coupling):
    modes_dev, rows, cols = source_field.shape
    n = lax.axis_size("mode")
    modes = targets.shape[0]
    terms = coeff_fields.shape[0]
    tiles = pltpu.VMEM((n * SUB, LANES), jnp.float32)
    grid_row = pltpu.VMEM((modes, cols), jnp.float32)
    image = jax.ShapeDtypeStruct(source_field.shape, jnp.float32)
    in_vmem = pl.BlockSpec(memory_space=pltpu.VMEM)
    in_hbm = pl.BlockSpec(memory_space=pltpu.HBM)
    table = (targets.shape[1], modes)
    dma = pltpu.SemaphoreType.DMA
    return pl.pallas_call(
        functools.partial(kernel, n, float(modes * rows * cols)),
        out_shape=(image, image),
        in_specs=[in_hbm] * 6,
        out_specs=(in_vmem, in_vmem),
        scratch_shapes=[
            pltpu.VMEM(source_field.shape, jnp.float32),
            pltpu.VMEM((terms, SUB, cols), jnp.float32),
            pltpu.VMEM(table, jnp.int32), pltpu.VMEM(table, jnp.int32),
            pltpu.VMEM(table, jnp.int32), pltpu.VMEM(table, jnp.float32),
        ]
        + [tiles] * 6
        + [
            pltpu.VMEM((1, LANES), jnp.float32),
            pltpu.VMEM((n, 1, LANES), jnp.float32),
            grid_row, grid_row, grid_row,
            pltpu.VMEM((terms * modes, 2 * modes), jnp.bfloat16),
            pltpu.VMEM((terms * modes, modes), jnp.bfloat16),
        ]
        + [dma] * 8 + [dma((2,)), dma((2,)), dma, dma((5,))],
        compiler_params=pltpu.CompilerParams(
            collective_id=0, has_side_effects=True, vmem_limit_bytes=60 * 1024 * 1024
        ),
    )(source_field, coeff_fields, targets.T, dest_slot.T, coef_mode.T, coupling.T)


def local(source_field, *rest):
    modes_dev, rows, cols = source_field.shape
    n = lax.axis_size("mode")
    if n == rows and n >= 16 and n & (n - 1) == 0 and cols % LANES == 0 and modes_dev * (cols // LANES) == SUB:
        return local_rows(source_field, *rest)
    return local_general(source_field, *rest)


def solution(mesh):
    in_specs = (P(("group", "mode"), None, None), P("group", None, None), P(), P(), P(), P())
    out_specs = (P(("group", "mode"), None, None), P(("group", "mode"), None, None))
    return jax.shard_map(local, mesh=mesh, in_specs=in_specs, out_specs=out_specs, check_vma=False)
```

```python
import functools

import jax
import jax.numpy as jnp
from jax import lax
from jax.experimental import pallas as pl
from jax.experimental.pallas import tpu as pltpu
from jax.sharding import PartitionSpec as P

LANES = 128
SUB = 8
MESH = pl.DeviceIdType.MESH


def laplace(fields):
    padded = jnp.pad(fields, ((0, 0), (1, 1), (1, 1)))
    return (
        4.0 * fields
        - padded[:, 2:, 1:-1]
        - padded[:, :-2, 1:-1]
        - padded[:, 1:-1, 2:]
        - padded[:, 1:-1, :-2]
    )


def local_general(source_field, coeff_fields, targets, dest_slot, coef_mode, coupling):
    local_modes, grid_rows, grid_cols = source_field.shape
    cell_count = grid_rows * grid_cols
    devices = lax.axis_size("mode")
    own_index = lax.axis_index("mode")
    coef_count = coeff_fields.shape[0]
    fan_out = targets.shape[1]
    entries = local_modes * fan_out
    slot_count = max(2, -(-entries // devices))
    highest = lax.Precision.HIGHEST
    flat_coeff = coeff_fields.reshape(coef_count, cell_count)
    mode_iota = jnp.arange(local_modes, dtype=jnp.int32)
    coef_iota = jnp.arange(coef_count, dtype=jnp.int32)
    owner_iota = jnp.arange(devices, dtype=jnp.int32)
    first_row = own_index * local_modes
    own_targets = lax.dynamic_slice_in_dim(targets, first_row, local_modes, 0).reshape(entries)
    own_coef = lax.dynamic_slice_in_dim(coef_mode, first_row, local_modes, 0).reshape(entries)
    own_value = lax.dynamic_slice_in_dim(coupling, first_row, local_modes, 0).reshape(entries)

    def local_products(fields):
        stencil = laplace(fields).reshape(local_modes, cell_count)
        coef_hot = (own_coef[:, None] == coef_iota[None, :]).astype(jnp.float32)
        picked = jnp.dot(coef_hot, flat_coeff, precision=highest)
        stencil_rows = jnp.repeat(stencil, fan_out, axis=0)
        return own_value[:, None] * stencil_rows * picked

    def apply_galerkin(fields):
        products = local_products(fields)
        owner_hot = (own_targets[:, None] == owner_iota[None, :]).astype(jnp.int32)
        slot_rank = jnp.sum((jnp.cumsum(owner_hot, axis=0) - owner_hot) * owner_hot, axis=1)
        slot_place = own_targets * slot_count + slot_rank
        packing = (
            jnp.arange(devices * slot_count, dtype=jnp.int32)[:, None] == slot_place[None, :]
        ).astype(jnp.float32)
        outgoing = jnp.dot(packing, products, precision=highest).reshape(
            devices, slot_count, cell_count
        )
        incoming = lax.all_to_all(outgoing, "mode", split_axis=0, concat_axis=0, tiled=True)
        all_targets = targets.reshape(devices, entries)
        all_dest = dest_slot.reshape(devices, entries)
        all_hot = (all_targets[..., None] == owner_iota).astype(jnp.int32)
        all_rank = jnp.sum((jnp.cumsum(all_hot, axis=1) - all_hot) * all_hot, axis=2)
        owned_here = (all_targets == own_index).astype(jnp.float32)
        dest_hot = (all_dest[..., None] == mode_iota).astype(jnp.float32) * owned_here[..., None]
        rank_hot = (all_rank[..., None] == jnp.arange(slot_count, dtype=jnp.int32)).astype(
            jnp.float32
        )
        collect = jnp.einsum("sem,sec->msc", dest_hot, rank_hot, precision=highest)
        collect = collect.reshape(local_modes, devices * slot_count)
        result = jnp.dot(
            collect, incoming.reshape(devices * slot_count, cell_count), precision=highest
        )
        return result.reshape(local_modes, grid_rows, grid_cols)

    energy = lax.psum(jnp.sum(source_field * source_field), "mode")
    field_scale = jnp.sqrt(energy / (targets.shape[0] * cell_count) + 1e-06)
    start_field = source_field / field_scale
    first_image = apply_galerkin(start_field)
    second_image = apply_galerkin(first_image)
    return (first_image, second_image)


def row_of(device):
    core = device % 2
    chip = device // 2
    x = chip % 2
    y = (chip // 2) % 2
    z = chip // 4
    place = y * 2 + (x + y) % 2
    odd = z % 2
    place = place + odd * (3 - 2 * place)
    return (z * 4 + place) * 2 + core


def device_of(row):
    core = row % 2
    step = row // 2
    z = step // 4
    place = step % 4
    odd = z % 2
    place = place + odd * (3 - 2 * place)
    y = place // 2
    x = (place + y) % 2
    return ((z * 2 + y) * 2 + x) * 2 + core


def split(values):
    high = values.astype(jnp.bfloat16)
    return high, (values - high.astype(jnp.float32)).astype(jnp.bfloat16)


def side_sum(field):
    cols = field.shape[1]
    place = lax.broadcasted_iota(jnp.int32, field.shape, 1)
    left = jnp.where(place == 0, 0.0, pltpu.roll(field, 1, 1))
    right = jnp.where(place == cols - 1, 0.0, pltpu.roll(field, cols - 1, 1))
    return left + right


def end_sum(field):
    rows = field.shape[0]
    place = lax.broadcasted_iota(jnp.int32, field.shape, 0)
    upper = jnp.where(place == 0, 0.0, pltpu.roll(field, 1, 0))
    lower = jnp.where(place == rows - 1, 0.0, pltpu.roll(field, rows - 1, 0))
    return upper + lower


def kernel(
    n, cell_total,
    source_hbm, coeff_hbm, targets_hbm, dest_hbm, coef_mode_hbm, coupling_hbm,
    first, second,
    source, coeff, targets, dest, coef_mode, coupling,
    out_a, in_a, out_b, in_b, out_c, in_c, e_out, e_in, mine, above, below, a_high, a_low,
    send_a, recv_a, send_b, recv_b, send_c, recv_c, send_e, recv_e, send_h, recv_h, load_source, load_rest,
):
    modes_dev, rows, cols = source.shape
    terms = coeff.shape[0]
    top, modes = targets.shape
    halves = cols // LANES
    me = lax.axis_index("mode")
    row = row_of(me)
    block = pl.multiple_of(row // SUB * SUB, SUB)

    loads = [pltpu.make_async_copy(source_hbm, source, load_source)]
    pairs = (
        (targets_hbm, targets), (dest_hbm, dest), (coef_mode_hbm, coef_mode), (coupling_hbm, coupling),
        (coeff_hbm.at[:, pl.ds(block, SUB), :], coeff),
    )
    loads += [pltpu.make_async_copy(src, dst, load_rest.at[k]) for k, (src, dst) in enumerate(pairs)]
    for load in loads:
        load.start()

    barrier = pltpu.get_barrier_semaphore()

    def greet(step, _):
        pl.semaphore_signal(
            barrier, inc=1, device_id={"mode": lax.rem(me + step, n)}, device_id_type=MESH
        )
        return 0

    lax.fori_loop(1, n, greet, 0)

    def tile(buf, index):
        return buf.at[pl.ds(pl.multiple_of(index * SUB, SUB), SUB), :]

    loads[0].wait()
    energy = jnp.zeros((1, LANES), jnp.float32)
    for m in range(modes_dev):
        field = source[m]
        stencil = 4.0 * field - end_sum(field) - side_sum(field)
        squares = jnp.sum(field * field, axis=0, keepdims=True)
        for h in range(halves):
            out_a[pl.ds(h * modes_dev + m, rows, stride=SUB), :] = stencil[:, h * LANES:(h + 1) * LANES]
            energy = energy + squares[:, h * LANES:(h + 1) * LANES]
    e_out[...] = energy

    pl.semaphore_wait(barrier, n - 1)

    def send_rows(step, _):
        other = lax.rem(me + step, n)
        pltpu.make_async_remote_copy(
            src_ref=tile(out_a, row_of(other)), dst_ref=tile(in_a, me),
            send_sem=send_a, recv_sem=recv_a,
            device_id={"mode": other}, device_id_type=MESH,
        ).start()
        return 0

    def send_energy(step, _):
        other = lax.rem(me + step, n)
        pltpu.make_async_remote_copy(
            src_ref=e_out, dst_ref=e_in.at[me],
            send_sem=send_e, recv_sem=recv_e,
            device_id={"mode": other}, device_id_type=MESH,
        ).start()
        return 0

    lax.fori_loop(1, n, send_rows, 0)
    e_in[me] = energy
    in_a[pl.ds(pl.multiple_of(me * SUB, SUB), SUB), :] = out_a[pl.ds(pl.multiple_of(row * SUB, SUB), SUB), :]

    for load in loads[1:]:
        load.wait()
    j_iota = lax.broadcasted_iota(jnp.int32, (modes, modes), 0)
    p_iota = lax.broadcasted_iota(jnp.int32, (modes, modes), 1)
    order = jnp.where((j_iota % modes_dev) * n + j_iota // modes_dev == p_iota, 1.0, 0.0)

    def reordered(values):
        return lax.dot_general(
            values, order, (((1,), (0,)), ((), ())),
            precision=lax.Precision.HIGHEST, preferred_element_type=jnp.float32,
        )

    place_t = reordered((dest[...] * n + targets[...]).astype(jnp.float32))
    coef_t = reordered(coef_mode[...].astype(jnp.float32))
    value_t = reordered(coupling[...])
    k_iota = j_iota.astype(jnp.float32)
    value = jnp.zeros((modes, modes), jnp.float32)
    index = jnp.zeros((modes, modes), jnp.float32)
    for t in range(top):
        hit = place_t[t:t + 1, :] == k_iota
        value = jnp.where(hit, value_t[t:t + 1, :], value)
        index = jnp.where(hit, coef_t[t:t + 1, :], index)
    for i in range(terms):
        high, low = split(jnp.where(index == float(i), value, 0.0))
        rows_i = pl.ds(i * modes, modes)
        a_high[rows_i, :modes] = high
        a_high[rows_i, modes:] = high
        a_low[rows_i, :] = low

    def galerkin(stencil):
        high, low = split(stencil)
        both = jnp.concatenate([high, low], axis=0)
        total = jnp.zeros((modes, cols), jnp.float32)
        for i in range(terms):
            rows_i = pl.ds(i * modes, modes)
            mixture = jnp.dot(a_high[rows_i, :], both, preferred_element_type=jnp.float32)
            mixture = mixture + jnp.dot(a_low[rows_i, :], high, preferred_element_type=jnp.float32)
            total = total + coeff[i, pl.ds(row - block, 1), :] * mixture
        return total

    def wait_all(out_buf, in_buf, send, recv):
        count = pl.ds(0, (n - 1) * SUB)
        pltpu.make_async_copy(out_buf.at[count, :], out_buf.at[count, :], send).wait()
        pltpu.make_async_copy(in_buf.at[count, :], in_buf.at[count, :], recv).wait()

    wait_all(out_a, in_a, send_a, recv_a)
    stencil = jnp.concatenate(
        [
            jnp.concatenate(
                [in_a[pl.ds(h * modes_dev + m, n, stride=SUB), :] for h in range(halves)], axis=1
            )
            for m in range(modes_dev)
        ],
        axis=0,
    )
    image = galerkin(stencil)
    mine[...] = image

    def halo(there, slot, sem):
        return pltpu.make_async_remote_copy(
            src_ref=mine, dst_ref=slot, send_sem=send_h.at[sem], recv_sem=recv_h.at[sem],
            device_id={"mode": device_of(there)}, device_id_type=MESH,
        )

    @pl.when(row < rows - 1)
    def _():
        halo(row + 1, above, 0).start()

    @pl.when(row > 0)
    def _():
        halo(row - 1, below, 1).start()

    def place_tiles(buf, values):
        for m in range(modes_dev):
            for h in range(halves):
                buf[pl.ds(h * modes_dev + m, n, stride=SUB), :] = values[
                    m * n:(m + 1) * n, h * LANES:(h + 1) * LANES
                ]

    def send_back(out_buf, in_buf, send, recv):
        def body(step, _):
            other = lax.rem(me + step, n)
            pltpu.make_async_remote_copy(
                src_ref=tile(out_buf, other), dst_ref=tile(in_buf, row),
                send_sem=send, recv_sem=recv,
                device_id={"mode": other}, device_id_type=MESH,
            ).start()
            return 0

        lax.fori_loop(1, n, body, 0)
        in_buf[pl.ds(pl.multiple_of(row * SUB, SUB), SUB), :] = out_buf[
            pl.ds(pl.multiple_of(me * SUB, SUB), SUB), :
        ]

    def take_tiles(buf, result):
        for m in range(modes_dev):
            for h in range(halves):
                result[m, :, h * LANES:(h + 1) * LANES] = buf[
                    pl.ds(h * modes_dev + m, rows, stride=SUB), :
                ] * scale

    place_tiles(out_b, image)
    send_back(out_b, in_b, send_b, recv_b)

    lax.fori_loop(1, n, send_energy, 0)
    inner = 4.0 * image - side_sum(image)

    @pl.when(row == 0)
    def _():
        above[...] = jnp.zeros_like(above)

    @pl.when(row == rows - 1)
    def _():
        below[...] = jnp.zeros_like(below)

    @pl.when(row > 0)
    def _():
        halo(row - 1, above, 0).wait_recv()

    @pl.when(row < rows - 1)
    def _():
        halo(row + 1, below, 1).wait_recv()

    image = galerkin(inner - above[...] - below[...])
    place_tiles(out_c, image)
    send_back(out_c, in_c, send_c, recv_c)

    wait_all(out_b, in_b, send_b, recv_b)
    others = pl.ds(0, n - 1)
    pltpu.make_async_copy(e_in.at[others], e_in.at[others], recv_e).wait()
    pltpu.make_async_copy(e_in.at[others], e_in.at[others], send_e).wait()
    whole = jnp.sum(jnp.sum(e_in[...], axis=0), axis=1, keepdims=True)
    scale = 1.0 / jnp.sqrt(whole / cell_total + 1e-06)
    take_tiles(in_b, first)

    @pl.when(row < rows - 1)
    def _():
        halo(row + 1, above, 0).wait_send()

    @pl.when(row > 0)
    def _():
        halo(row - 1, below, 1).wait_send()

    wait_all(out_c, in_c, send_c, recv_c)
    take_tiles(in_c, second)


def local_rows(source_field, coeff_fields, targets, dest_slot, coef_mode, coupling):
    modes_dev, rows, cols = source_field.shape
    n = lax.axis_size("mode")
    modes = targets.shape[0]
    terms = coeff_fields.shape[0]
    tiles = pltpu.VMEM((n * SUB, LANES), jnp.float32)
    grid_row = pltpu.VMEM((modes, cols), jnp.float32)
    image = jax.ShapeDtypeStruct(source_field.shape, jnp.float32)
    in_vmem = pl.BlockSpec(memory_space=pltpu.VMEM)
    in_hbm = pl.BlockSpec(memory_space=pltpu.HBM)
    table = (targets.shape[1], modes)
    dma = pltpu.SemaphoreType.DMA
    return pl.pallas_call(
        functools.partial(kernel, n, float(modes * rows * cols)),
        out_shape=(image, image),
        in_specs=[in_hbm] * 6,
        out_specs=(in_vmem, in_vmem),
        scratch_shapes=[
            pltpu.VMEM(source_field.shape, jnp.float32),
            pltpu.VMEM((terms, SUB, cols), jnp.float32),
            pltpu.VMEM(table, jnp.int32), pltpu.VMEM(table, jnp.int32),
            pltpu.VMEM(table, jnp.int32), pltpu.VMEM(table, jnp.float32),
        ]
        + [tiles] * 6
        + [
            pltpu.VMEM((1, LANES), jnp.float32),
            pltpu.VMEM((n, 1, LANES), jnp.float32),
            grid_row, grid_row, grid_row,
            pltpu.VMEM((terms * modes, 2 * modes), jnp.bfloat16),
            pltpu.VMEM((terms * modes, modes), jnp.bfloat16),
        ]
        + [dma] * 8 + [dma((2,)), dma((2,)), dma, dma((5,))],
        compiler_params=pltpu.CompilerParams(
            collective_id=0, has_side_effects=True, vmem_limit_bytes=32 * 1024 * 1024
        ),
    )(*[
        pltpu.with_memory_space_constraint(value, pltpu.HBM)
        for value in (source_field, coeff_fields, targets.T, dest_slot.T, coef_mode.T, coupling.T)
    ])


def local(source_field, *rest):
    modes_dev, rows, cols = source_field.shape
    n = lax.axis_size("mode")
    if n == rows and n >= 16 and n & (n - 1) == 0 and cols % LANES == 0 and modes_dev * (cols // LANES) == SUB:
        return local_rows(source_field, *rest)
    return local_general(source_field, *rest)


def solution(mesh):
    in_specs = (P(("group", "mode"), None, None), P("group", None, None), P(), P(), P(), P())
    out_specs = (P(("group", "mode"), None, None), P(("group", "mode"), None, None))
    return jax.shard_map(local, mesh=mesh, in_specs=in_specs, out_specs=out_specs, check_vma=False)
```

```python
import functools

import jax
import jax.numpy as jnp
from jax import lax
from jax.experimental import pallas as pl
from jax.experimental.pallas import tpu as pltpu
from jax.sharding import PartitionSpec as P

LANES = 128
SUB = 8
MESH = pl.DeviceIdType.MESH


def laplace(fields):
    padded = jnp.pad(fields, ((0, 0), (1, 1), (1, 1)))
    return (
        4.0 * fields
        - padded[:, 2:, 1:-1]
        - padded[:, :-2, 1:-1]
        - padded[:, 1:-1, 2:]
        - padded[:, 1:-1, :-2]
    )


def local_general(source_field, coeff_fields, targets, dest_slot, coef_mode, coupling):
    local_modes, grid_rows, grid_cols = source_field.shape
    cell_count = grid_rows * grid_cols
    devices = lax.axis_size("mode")
    own_index = lax.axis_index("mode")
    coef_count = coeff_fields.shape[0]
    fan_out = targets.shape[1]
    entries = local_modes * fan_out
    slot_count = max(2, -(-entries // devices))
    highest = lax.Precision.HIGHEST
    flat_coeff = coeff_fields.reshape(coef_count, cell_count)
    mode_iota = jnp.arange(local_modes, dtype=jnp.int32)
    coef_iota = jnp.arange(coef_count, dtype=jnp.int32)
    owner_iota = jnp.arange(devices, dtype=jnp.int32)
    first_row = own_index * local_modes
    own_targets = lax.dynamic_slice_in_dim(targets, first_row, local_modes, 0).reshape(entries)
    own_coef = lax.dynamic_slice_in_dim(coef_mode, first_row, local_modes, 0).reshape(entries)
    own_value = lax.dynamic_slice_in_dim(coupling, first_row, local_modes, 0).reshape(entries)

    def local_products(fields):
        stencil = laplace(fields).reshape(local_modes, cell_count)
        coef_hot = (own_coef[:, None] == coef_iota[None, :]).astype(jnp.float32)
        picked = jnp.dot(coef_hot, flat_coeff, precision=highest)
        stencil_rows = jnp.repeat(stencil, fan_out, axis=0)
        return own_value[:, None] * stencil_rows * picked

    def apply_galerkin(fields):
        products = local_products(fields)
        owner_hot = (own_targets[:, None] == owner_iota[None, :]).astype(jnp.int32)
        slot_rank = jnp.sum((jnp.cumsum(owner_hot, axis=0) - owner_hot) * owner_hot, axis=1)
        slot_place = own_targets * slot_count + slot_rank
        packing = (
            jnp.arange(devices * slot_count, dtype=jnp.int32)[:, None] == slot_place[None, :]
        ).astype(jnp.float32)
        outgoing = jnp.dot(packing, products, precision=highest).reshape(
            devices, slot_count, cell_count
        )
        incoming = lax.all_to_all(outgoing, "mode", split_axis=0, concat_axis=0, tiled=True)
        all_targets = targets.reshape(devices, entries)
        all_dest = dest_slot.reshape(devices, entries)
        all_hot = (all_targets[..., None] == owner_iota).astype(jnp.int32)
        all_rank = jnp.sum((jnp.cumsum(all_hot, axis=1) - all_hot) * all_hot, axis=2)
        owned_here = (all_targets == own_index).astype(jnp.float32)
        dest_hot = (all_dest[..., None] == mode_iota).astype(jnp.float32) * owned_here[..., None]
        rank_hot = (all_rank[..., None] == jnp.arange(slot_count, dtype=jnp.int32)).astype(
            jnp.float32
        )
        collect = jnp.einsum("sem,sec->msc", dest_hot, rank_hot, precision=highest)
        collect = collect.reshape(local_modes, devices * slot_count)
        result = jnp.dot(
            collect, incoming.reshape(devices * slot_count, cell_count), precision=highest
        )
        return result.reshape(local_modes, grid_rows, grid_cols)

    energy = lax.psum(jnp.sum(source_field * source_field), "mode")
    field_scale = jnp.sqrt(energy / (targets.shape[0] * cell_count) + 1e-06)
    start_field = source_field / field_scale
    first_image = apply_galerkin(start_field)
    second_image = apply_galerkin(first_image)
    return (first_image, second_image)


def row_of(device):
    core = device % 2
    chip = device // 2
    x = chip % 2
    y = (chip // 2) % 2
    z = chip // 4
    place = y * 2 + (x + y) % 2
    odd = z % 2
    place = place + odd * (3 - 2 * place)
    return (z * 4 + place) * 2 + core


def device_of(row):
    core = row % 2
    step = row // 2
    z = step // 4
    place = step % 4
    odd = z % 2
    place = place + odd * (3 - 2 * place)
    y = place // 2
    x = (place + y) % 2
    return ((z * 2 + y) * 2 + x) * 2 + core


def split(values):
    high = values.astype(jnp.bfloat16)
    return high, (values - high.astype(jnp.float32)).astype(jnp.bfloat16)


def side_sum(field):
    cols = field.shape[1]
    place = lax.broadcasted_iota(jnp.int32, field.shape, 1)
    left = jnp.where(place == 0, 0.0, pltpu.roll(field, 1, 1))
    right = jnp.where(place == cols - 1, 0.0, pltpu.roll(field, cols - 1, 1))
    return left + right


def end_sum(field):
    rows = field.shape[0]
    place = lax.broadcasted_iota(jnp.int32, field.shape, 0)
    upper = jnp.where(place == 0, 0.0, pltpu.roll(field, 1, 0))
    lower = jnp.where(place == rows - 1, 0.0, pltpu.roll(field, rows - 1, 0))
    return upper + lower


def kernel(
    n, cell_total,
    source_hbm, coeff_hbm, targets_hbm, dest_hbm, coef_mode_hbm, coupling_hbm,
    first, second,
    source, coeff, targets, dest, coef_mode, coupling,
    out_a, in_a, out_b, in_b, out_c, in_c, e_out, e_in, mine, above, below, a_high, a_low,
    send_a, recv_a, send_b, recv_b, send_c, recv_c, send_e, recv_e, send_h, recv_h, load_source, load_rest,
):
    modes_dev, rows, cols = source.shape
    terms = coeff.shape[0]
    top, modes = targets.shape
    halves = cols // LANES
    me = lax.axis_index("mode")
    row = row_of(me)
    block = pl.multiple_of(row // SUB * SUB, SUB)

    loads = [pltpu.make_async_copy(source_hbm, source, load_source)]
    pairs = (
        (targets_hbm, targets), (dest_hbm, dest), (coef_mode_hbm, coef_mode), (coupling_hbm, coupling),
        (coeff_hbm.at[:, pl.ds(block, SUB), :], coeff),
    )
    loads += [pltpu.make_async_copy(src, dst, load_rest.at[k]) for k, (src, dst) in enumerate(pairs)]
    for load in loads:
        load.start()

    barrier = pltpu.get_barrier_semaphore()

    def greet(step, _):
        pl.semaphore_signal(
            barrier, inc=1, device_id={"mode": lax.rem(me + step, n)}, device_id_type=MESH
        )
        return 0

    lax.fori_loop(1, n, greet, 0)

    def tile(buf, index):
        return buf.at[pl.ds(pl.multiple_of(index * SUB, SUB), SUB), :]

    loads[0].wait()
    energy = jnp.zeros((1, LANES), jnp.float32)
    for m in range(modes_dev):
        field = source[m]
        stencil = 4.0 * field - end_sum(field) - side_sum(field)
        squares = jnp.sum(field * field, axis=0, keepdims=True)
        for h in range(halves):
            out_a[pl.ds(h * modes_dev + m, rows, stride=SUB), :] = stencil[:, h * LANES:(h + 1) * LANES]
            energy = energy + squares[:, h * LANES:(h + 1) * LANES]
    e_out[...] = energy

    pl.semaphore_wait(barrier, n - 1)

    def send_rows(step, _):
        other = lax.rem(me + step, n)
        pltpu.make_async_remote_copy(
            src_ref=tile(out_a, row_of(other)), dst_ref=tile(in_a, me),
            send_sem=send_a, recv_sem=recv_a,
            device_id={"mode": other}, device_id_type=MESH,
        ).start()
        return 0

    def send_energy(step, _):
        other = lax.rem(me + step, n)
        pltpu.make_async_remote_copy(
            src_ref=e_out, dst_ref=e_in.at[me],
            send_sem=send_e, recv_sem=recv_e,
            device_id={"mode": other}, device_id_type=MESH,
        ).start()
        return 0

    lax.fori_loop(1, n, send_rows, 0)
    e_in[me] = energy
    in_a[pl.ds(pl.multiple_of(me * SUB, SUB), SUB), :] = out_a[pl.ds(pl.multiple_of(row * SUB, SUB), SUB), :]

    for load in loads[1:]:
        load.wait()
    j_iota = lax.broadcasted_iota(jnp.int32, (modes, modes), 0)
    p_iota = lax.broadcasted_iota(jnp.int32, (modes, modes), 1)
    order = jnp.where((j_iota % modes_dev) * n + j_iota // modes_dev == p_iota, 1.0, 0.0)

    def reordered(values):
        return lax.dot_general(
            values, order, (((1,), (0,)), ((), ())),
            precision=lax.Precision.HIGHEST, preferred_element_type=jnp.float32,
        )

    place_t = reordered((dest[...] * n + targets[...]).astype(jnp.float32))
    coef_t = reordered(coef_mode[...].astype(jnp.float32))
    value_t = reordered(coupling[...])
    k_iota = j_iota.astype(jnp.float32)
    value = jnp.zeros((modes, modes), jnp.float32)
    index = jnp.zeros((modes, modes), jnp.float32)
    for t in range(top):
        hit = place_t[t:t + 1, :] == k_iota
        value = jnp.where(hit, value_t[t:t + 1, :], value)
        index = jnp.where(hit, coef_t[t:t + 1, :], index)
    for i in range(terms):
        high, low = split(jnp.where(index == float(i), value, 0.0))
        rows_i = pl.ds(i * modes, modes)
        a_high[rows_i, :modes] = high
        a_high[rows_i, modes:] = high
        a_low[rows_i, :] = low

    def galerkin(stencil):
        high, low = split(stencil)
        both = jnp.concatenate([high, low], axis=0)
        total = jnp.zeros((modes, cols), jnp.float32)
        for i in range(terms):
            rows_i = pl.ds(i * modes, modes)
            mixture = jnp.dot(a_high[rows_i, :], both, preferred_element_type=jnp.float32)
            mixture = mixture + jnp.dot(a_low[rows_i, :], high, preferred_element_type=jnp.float32)
            total = total + coeff[i, pl.ds(row - block, 1), :] * mixture
        return total

    def wait_bytes(buf, sem):
        count = pl.ds(0, (n - 1) * SUB)
        pltpu.make_async_copy(buf.at[count, :], buf.at[count, :], sem).wait()

    wait_bytes(in_a, recv_a)
    stencil = jnp.concatenate(
        [
            jnp.concatenate(
                [in_a[pl.ds(h * modes_dev + m, n, stride=SUB), :] for h in range(halves)], axis=1
            )
            for m in range(modes_dev)
        ],
        axis=0,
    )
    image = galerkin(stencil)
    mine[...] = image

    def halo(there, slot, sem):
        return pltpu.make_async_remote_copy(
            src_ref=mine, dst_ref=slot, send_sem=send_h.at[sem], recv_sem=recv_h.at[sem],
            device_id={"mode": device_of(there)}, device_id_type=MESH,
        )

    @pl.when(row < rows - 1)
    def _():
        halo(row + 1, above, 0).start()

    @pl.when(row > 0)
    def _():
        halo(row - 1, below, 1).start()

    def place_tiles(buf, values):
        for m in range(modes_dev):
            for h in range(halves):
                buf[pl.ds(h * modes_dev + m, n, stride=SUB), :] = values[
                    m * n:(m + 1) * n, h * LANES:(h + 1) * LANES
                ]

    def send_back(out_buf, in_buf, send, recv):
        def body(step, _):
            other = lax.rem(me + step, n)
            pltpu.make_async_remote_copy(
                src_ref=tile(out_buf, other), dst_ref=tile(in_buf, row),
                send_sem=send, recv_sem=recv,
                device_id={"mode": other}, device_id_type=MESH,
            ).start()
            return 0

        lax.fori_loop(1, n, body, 0)
        in_buf[pl.ds(pl.multiple_of(row * SUB, SUB), SUB), :] = out_buf[
            pl.ds(pl.multiple_of(me * SUB, SUB), SUB), :
        ]

    def take_tiles(buf, result):
        for m in range(modes_dev):
            for h in range(halves):
                result[m, :, h * LANES:(h + 1) * LANES] = buf[
                    pl.ds(h * modes_dev + m, rows, stride=SUB), :
                ] * scale

    place_tiles(out_b, image)
    send_back(out_b, in_b, send_b, recv_b)

    lax.fori_loop(1, n, send_energy, 0)
    inner = 4.0 * image - side_sum(image)

    @pl.when(row == 0)
    def _():
        above[...] = jnp.zeros_like(above)

    @pl.when(row == rows - 1)
    def _():
        below[...] = jnp.zeros_like(below)

    @pl.when(row > 0)
    def _():
        halo(row - 1, above, 0).wait_recv()

    @pl.when(row < rows - 1)
    def _():
        halo(row + 1, below, 1).wait_recv()

    image = galerkin(inner - above[...] - below[...])
    place_tiles(out_c, image)
    send_back(out_c, in_c, send_c, recv_c)

    wait_bytes(in_b, recv_b)
    others = pl.ds(0, n - 1)
    pltpu.make_async_copy(e_in.at[others], e_in.at[others], recv_e).wait()
    pltpu.make_async_copy(e_in.at[others], e_in.at[others], send_e).wait()
    whole = jnp.sum(jnp.sum(e_in[...], axis=0), axis=1, keepdims=True)
    scale = 1.0 / jnp.sqrt(whole / cell_total + 1e-06)
    take_tiles(in_b, first)

    @pl.when(row < rows - 1)
    def _():
        halo(row + 1, above, 0).wait_send()

    @pl.when(row > 0)
    def _():
        halo(row - 1, below, 1).wait_send()

    wait_bytes(in_c, recv_c)
    take_tiles(in_c, second)
    for buf, sem in ((out_a, send_a), (out_b, send_b), (out_c, send_c)):
        wait_bytes(buf, sem)


def local_rows(source_field, coeff_fields, targets, dest_slot, coef_mode, coupling):
    modes_dev, rows, cols = source_field.shape
    n = lax.axis_size("mode")
    modes = targets.shape[0]
    terms = coeff_fields.shape[0]
    tiles = pltpu.VMEM((n * SUB, LANES), jnp.float32)
    grid_row = pltpu.VMEM((modes, cols), jnp.float32)
    image = jax.ShapeDtypeStruct(source_field.shape, jnp.float32)
    in_vmem = pl.BlockSpec(memory_space=pltpu.VMEM)
    in_hbm = pl.BlockSpec(memory_space=pltpu.HBM)
    table = (targets.shape[1], modes)
    dma = pltpu.SemaphoreType.DMA
    return pl.pallas_call(
        functools.partial(kernel, n, float(modes * rows * cols)),
        out_shape=(image, image),
        in_specs=[in_hbm] * 6,
        out_specs=(in_vmem, in_vmem),
        scratch_shapes=[
            pltpu.VMEM(source_field.shape, jnp.float32),
            pltpu.VMEM((terms, SUB, cols), jnp.float32),
            pltpu.VMEM(table, jnp.int32), pltpu.VMEM(table, jnp.int32),
            pltpu.VMEM(table, jnp.int32), pltpu.VMEM(table, jnp.float32),
        ]
        + [tiles] * 6
        + [
            pltpu.VMEM((1, LANES), jnp.float32),
            pltpu.VMEM((n, 1, LANES), jnp.float32),
            grid_row, grid_row, grid_row,
            pltpu.VMEM((terms * modes, 2 * modes), jnp.bfloat16),
            pltpu.VMEM((terms * modes, modes), jnp.bfloat16),
        ]
        + [dma] * 8 + [dma((2,)), dma((2,)), dma, dma((5,))],
        compiler_params=pltpu.CompilerParams(
            collective_id=0, has_side_effects=True, vmem_limit_bytes=32 * 1024 * 1024
        ),
    )(*[
        pltpu.with_memory_space_constraint(value, pltpu.HBM)
        for value in (source_field, coeff_fields, targets.T, dest_slot.T, coef_mode.T, coupling.T)
    ])


def local(source_field, *rest):
    modes_dev, rows, cols = source_field.shape
    n = lax.axis_size("mode")
    if n == rows and n >= 16 and n & (n - 1) == 0 and cols % LANES == 0 and modes_dev * (cols // LANES) == SUB:
        return local_rows(source_field, *rest)
    return local_general(source_field, *rest)


def solution(mesh):
    in_specs = (P(("group", "mode"), None, None), P("group", None, None), P(), P(), P(), P())
    out_specs = (P(("group", "mode"), None, None), P(("group", "mode"), None, None))
    return jax.shard_map(local, mesh=mesh, in_specs=in_specs, out_specs=out_specs, check_vma=False)
```
